512 devices in a mesh: wide: 64 (over x, z_hi, y), narrow: 8 (over z_lo, core).
Axes of the slice: x: 4, y: 8, z: 8 (z_hi: 2, z_lo: 4; z = z_hi * 4 + z_lo), core: 2. Of those that a mesh axis runs over, the one named last changes fastest.
Arguments:
- pooled: bfloat16 [9216, 8, 64, 128], P(None, 'narrow', 'wide'), may hold values from -6 to 6
- w_top: bfloat16 [8, 4096, 512], P('narrow', 'wide'), may hold values from -0.03125 to 0.03125
- bias: float32 [512], replicated, may hold values from -4 to 4
- grad_hidden: bfloat16 [9216, 512], P('wide', 'narrow'), may hold values from -6 to 6
Outputs:
- hidden: bfloat16 [9216, 512], P('wide', 'narrow')
- grad_pooled: bfloat16 [9216, 8, 64, 128], P('wide', 'narrow')
The draws below stay inside these ranges and needn't reach their ends.
All inputs are finite; a program needn't handle non-finite values.
Results may differ from the reference program's by a relative error of at most 0.009.
Values may be sent and summed in bfloat16 or wider, within the bound.
No kernel may reach another device: no remote copies, remote signals or barrier semaphores. Data moves between devices by JAX's collectives and lax.ppermute only.
A program may use at most 64 MiB of HBM per device.

```python
import jax
import jax.numpy as jnp

FB = 64
E = 128
H = 512
NB = 8
SAMPLES = 9216


def level_of(stream_key, extent, shards, least, top_value):
    loudness = 1.0
    for axis_at, blocks in shards:
        draws = jax.random.uniform(jax.random.fold_in(jax.random.fold_in(stream_key, 6), axis_at), (blocks,), jnp.float32, least / len(shards), top_value / len(shards))
        loudness = loudness * jnp.repeat(jnp.exp(draws), extent[axis_at] // blocks).reshape((-1,) + (1,) * (len(extent) - 1 - axis_at))
    return loudness


def bell_draw(stream_key, dims, scale, most, split=(), kind=jnp.bfloat16):
    factor_of = level_of(stream_key, dims, split, -0.22, 0.18) if split else 1.0
    entries = jax.random.normal(stream_key, dims, jnp.float32) * scale * factor_of
    return jnp.minimum(jnp.maximum(entries, -most), most).astype(kind)


def setup_inputs(seed: int = 0) -> dict:
    splits = jax.random.split(jax.random.key(seed), 5)
    pooled = bell_draw(splits[0], (SAMPLES, NB, FB, E), 1.0, 6.0, ((1, 8), (2, 64)))
    w_top = bell_draw(splits[1], (NB, FB * FB, H), (NB * FB * FB) ** -0.5, 0.03125, ((0, 8), (1, 64)))
    bias = bell_draw(splits[2], (H,), 0.7, 4.0, (), jnp.float32)
    grad_hidden = bell_draw(splits[3], (SAMPLES, H), 1.0, 6.0, ((0, 64), (1, 8)))
    return dict(pooled=pooled, w_top=w_top, bias=bias, grad_hidden=grad_hidden)


def gate_slope(pre_act):
    sigmoid_v = jax.nn.sigmoid(pre_act)
    return sigmoid_v * (1.0 + pre_act * (1.0 - sigmoid_v))


def reference(pooled, w_top, bias, grad_hidden):
    gram_scale = E ** -0.5
    sample_count = pooled.shape[0]
    pre_act = jnp.zeros((sample_count, H), jnp.float32) + bias.astype(jnp.float32)[None, :]
    for block in range(NB):
        paired = block ^ (NB // 2)
        mine_block = pooled[:, block].astype(jnp.float32)
        other_block = pooled[:, paired].astype(jnp.float32)
        gram_rows = (jnp.einsum("sie,sje->sij", mine_block, other_block) * gram_scale).astype(jnp.bfloat16)
        pre_act = pre_act + jnp.dot(gram_rows.reshape(sample_count, FB * FB), w_top[block], preferred_element_type=jnp.float32)
    hidden = jax.nn.silu(pre_act).astype(jnp.bfloat16)
    grad_pre = (grad_hidden.astype(jnp.float32) * gate_slope(pre_act)).astype(jnp.bfloat16)
    grad_grams = []
    for block in range(NB):
        grad_flat = jnp.dot(grad_pre, w_top[block].T, preferred_element_type=jnp.float32).astype(jnp.bfloat16)
        grad_grams.append(grad_flat.reshape(sample_count, FB, FB))
    pieces = []
    for block in range(NB):
        paired = block ^ (NB // 2)
        other_block = pooled[:, paired].astype(jnp.float32)
        direct_part = jnp.einsum("sij,sje->sie", grad_grams[block].astype(jnp.float32), other_block)
        mirror_part = jnp.einsum("sji,sje->sie", grad_grams[paired].astype(jnp.float32), other_block)
        pieces.append(((direct_part + mirror_part) * gram_scale).astype(jnp.bfloat16))
    grad_pooled = jnp.stack(pieces, axis=1)
    return hidden, grad_pooled
```

```python
import jax
import jax.numpy as jnp
from jax import lax
from jax.sharding import Mesh, PartitionSpec as P

X, ZH, Y = 4, 2, 8
BF = jnp.bfloat16
F32 = jnp.float32


def swap_block(v):
    return lax.ppermute(v, "nw", [(i, i ^ 4) for i in range(8)])


def cross_block(v):
    pairs = [(a * 8 + b, (a ^ 1) * 8 + (b ^ 4)) for a in range(ZH) for b in range(8)]
    return lax.ppermute(v, ("zh", "nw"), pairs)


def cross_same(v):
    return lax.ppermute(v, "zh", [(0, 1), (1, 0)])


def in_order(own, other, zh, axis):
    first = zh == 0
    return jnp.stack([jnp.where(first, own, other), jnp.where(first, other, own)], axis)


def folded_weights(w, zh):
    hidden = w.shape[-1]
    raw = w.reshape(X, ZH, Y, hidden)
    raw_other = cross_same(w).reshape(X, ZH, Y, hidden)
    mine = in_order(raw, raw_other, zh, 0)
    send = raw.transpose(0, 2, 1, 3).reshape(X * Y, ZH, hidden)
    turned = lax.all_to_all(send, ("x", "y"), 0, 0, tiled=True)
    near = swap_block(turned)
    far = cross_block(turned)
    theirs = in_order(near, far, zh, 0)
    theirs = theirs.reshape(ZH, X, Y, ZH, hidden).transpose(3, 1, 0, 2, 4)
    fold = (mine.astype(F32) + theirs.astype(F32)).astype(BF)
    fold = fold.reshape(ZH, 64, hidden)
    along_y = lax.all_gather(fold, "y", axis=1, tiled=False)
    along_x = lax.all_gather(along_y, "x", axis=0, tiled=False)
    return along_x.reshape(64 * 64, hidden)


def body(pooled, w_top, bias, grad_hidden):
    zh = lax.axis_index("zh")
    nw = lax.axis_index("nw")
    half = nw // 4
    count = pooled.shape[0] // (X * ZH * Y)
    hc = count // 2
    width = pooled.shape[-1]
    scale = width ** (-0.5)

    weights = folded_weights(w_top[0], zh)

    by_dest = pooled.reshape(X, ZH, Y, count, width).transpose(1, 0, 2, 3, 4)
    by_dest = by_dest.reshape(ZH, X * Y, count, width)
    mine = lax.dynamic_index_in_dim(by_dest, zh, 0, keepdims=False)
    theirs = lax.dynamic_index_in_dim(by_dest, 1 - zh, 0, keepdims=False)
    both = jnp.concatenate([mine, theirs], 1)
    both = lax.all_to_all(both, ("x", "y"), 0, 0, tiled=True)
    own = both[:, :count]
    away = both[:, count:]
    pair_own = swap_block(own)
    pair_away = cross_block(away)
    away_half = lax.dynamic_slice_in_dim(away, half * hc, hc, 1)
    same_away = cross_same(away_half)

    def fields(a, b):
        n = a.shape[1]
        v = in_order(a.reshape(X, Y, n, width), b.reshape(X, Y, n, width), zh, 1)
        return v.reshape(X * ZH * Y, n, width).transpose(1, 0, 2)

    left = fields(lax.dynamic_slice_in_dim(own, half * hc, hc, 1), same_away)
    right = fields(pair_own, pair_away)
    right_half = lax.dynamic_slice_in_dim(right, half * hc, hc, 0)
    gram = jnp.einsum("sie,sje->sij", left, right_half, preferred_element_type=F32)
    gram = (gram * scale).astype(BF).reshape(hc, 64 * 64)
    part = jnp.dot(gram, weights, preferred_element_type=F32).astype(BF)
    parts = lax.all_gather(part, "nw", axis=0, tiled=False)
    pre_act = parts.reshape(2, 4, hc, -1).astype(F32).sum(1).reshape(count, -1) + bias[None, :]

    share = grad_hidden.shape[1]
    mine_pre = lax.dynamic_slice_in_dim(pre_act, nw * share, share, 1)
    hidden = jax.nn.silu(mine_pre).astype(BF)
    cot = lax.all_gather(grad_hidden, "nw", axis=1, tiled=True)
    sig = jax.nn.sigmoid(pre_act)
    grad_pre = (cot.astype(F32) * (sig * (1.0 + pre_act * (1.0 - sig)))).astype(BF)
    both_grads = lax.dot_general(
        grad_pre, weights, (((1,), (1,)), ((), ())), preferred_element_type=F32
    )
    both_grads = both_grads.astype(BF).reshape(count, 64, 64)
    grad_pooled = jnp.einsum("sij,sje->sie", both_grads, right, preferred_element_type=F32)
    return hidden, (grad_pooled * scale).astype(BF)[:, None]


def solution(mesh):
    fine = Mesh(mesh.devices.reshape(X, ZH, Y, 8), ("x", "zh", "y", "nw"))
    wide = ("x", "zh", "y")
    in_specs = (P(None, "nw", wide, None), P("nw", wide, None), P(), P(wide, "nw"))
    out_specs = (P(wide, "nw"), P(wide, "nw", None, None))
    return jax.shard_map(body, mesh=fine, in_specs=in_specs, out_specs=out_specs, check_vma=False)
```

```python
import jax
import jax.numpy as jnp
from jax import lax
from jax.sharding import Mesh, PartitionSpec as P

X, ZH, Y = 4, 2, 8
XY = X * Y
CHUNKS = (16, 64, 64)
BF = jnp.bfloat16
F32 = jnp.float32


def swap_block(v):
    return lax.ppermute(v, "nw", [(i, i ^ 4) for i in range(8)])


def cross_block(v):
    pairs = [(a * 8 + b, (a ^ 1) * 8 + (b ^ 4)) for a in range(ZH) for b in range(8)]
    return lax.ppermute(v, ("zh", "nw"), pairs)


def cross_same(v):
    return lax.ppermute(v, "zh", [(0, 1), (1, 0)])


def in_order(own, other, zh, axis):
    first = zh == 0
    return jnp.stack([jnp.where(first, own, other), jnp.where(first, other, own)], axis)


def after(v, other, zh):
    return jnp.where(zh > 1, other[(0,) * other.ndim].astype(v.dtype), v)


def folded_weights(raw, raw_other, turned, zh):
    units = raw.shape[-1]
    mine = in_order(raw, raw_other, zh, 0)
    near = swap_block(turned)
    far = cross_block(turned)
    theirs = in_order(near, far, zh, 0).reshape(ZH, X, Y, ZH, units)
    theirs = theirs.transpose(3, 1, 0, 2, 4)
    fold = (mine.astype(F32) + theirs.astype(F32)).astype(BF)
    return fold.reshape(ZH * 64, units)


def body(pooled, w_top, bias, grad_hidden):
    zh = lax.axis_index("zh")
    nw = lax.axis_index("nw")
    half = nw // 4
    count = pooled.shape[0] // (XY * ZH)
    width = pooled.shape[-1]
    scale = width ** (-0.5)
    w = w_top[0]
    units = w.shape[-1]

    by_dest = pooled.reshape(X, ZH, Y, count, width).transpose(1, 0, 2, 3, 4)
    by_dest = by_dest.reshape(ZH, XY, count, width)
    mine = lax.dynamic_index_in_dim(by_dest, zh, 0, keepdims=False)
    theirs = lax.dynamic_index_in_dim(by_dest, 1 - zh, 0, keepdims=False)

    raw = w.reshape(X, ZH, Y, units)
    w_rows = raw.transpose(0, 2, 1, 3).reshape(XY, ZH * units // width, width)
    raw_other = cross_same(w).reshape(X, ZH, Y, units)
    cot = lax.all_gather(grad_hidden, "nw", axis=1, tiled=True)

    at = 0
    arrived = None
    lefts, rights, right_halves = [], [], []
    for index, n in enumerate(CHUNKS):
        pieces = [mine[:, at : at + n], theirs[:, at : at + n]]
        at += n
        if index == 0:
            pieces.append(w_rows)
        send = jnp.concatenate(pieces, 1)
        if arrived is not None:
            send = after(send, arrived, zh)
        got = lax.all_to_all(send, ("x", "y"), 0, 0, tiled=True)
        arrived = got
        if index == 0:
            turned = after(got[:, 2 * n :].reshape(XY, ZH, units), cot, zh)
            fold = folded_weights(raw, raw_other, turned, zh)
            weights = lax.all_gather(fold, ("x", "y"), axis=0, tiled=True)
        own, away = got[:, :n], got[:, n : 2 * n]
        pair_own = swap_block(own)
        pair_away = cross_block(away)
        h = n // 2
        same_away = cross_same(lax.dynamic_slice_in_dim(away, half * h, h, 1))

        def rows(a, b):
            m = a.shape[1]
            return in_order(a, b, zh, 1).reshape(XY * ZH, m, width).transpose(1, 0, 2)

        def columns(a, b):
            m = a.shape[1]
            v = in_order(a.reshape(X, Y, m, width), b.reshape(X, Y, m, width), zh, 1)
            return v.reshape(XY * ZH, m, width).transpose(1, 0, 2)

        lefts.append(rows(lax.dynamic_slice_in_dim(own, half * h, h, 1), same_away))
        right = columns(pair_own, pair_away)
        rights.append(right)
        right_halves.append(lax.dynamic_slice_in_dim(right, half * h, h, 0))

    left = jnp.concatenate(lefts, 0)
    right = jnp.concatenate(rights, 0)
    right_half = jnp.concatenate(right_halves, 0)
    hc = count // 2
    gram = jnp.einsum("sie,sje->sij", left, right_half, preferred_element_type=F32)
    gram = (gram * scale).astype(BF).reshape(hc, 64 * 64)
    part = jnp.dot(gram, weights, preferred_element_type=F32).astype(BF)
    parts = lax.all_gather(part, "nw", axis=0, tiled=False)
    sums = parts.reshape(2, 4, hc, units).astype(F32).sum(1)
    ordered = []
    at = 0
    for n in CHUNKS:
        h = n // 2
        ordered += [sums[0, at : at + h], sums[1, at : at + h]]
        at += h
    pre_act = jnp.concatenate(ordered, 0) + bias[None, :]

    share = grad_hidden.shape[1]
    mine_pre = lax.dynamic_slice_in_dim(pre_act, nw * share, share, 1)
    hidden = jax.nn.silu(mine_pre).astype(BF)
    sig = jax.nn.sigmoid(pre_act)
    grad_pre = (cot.astype(F32) * (sig * (1.0 + pre_act * (1.0 - sig)))).astype(BF)
    both_grads = lax.dot_general(
        grad_pre, weights, (((1,), (1,)), ((), ())), preferred_element_type=F32
    )
    both_grads = both_grads.astype(BF).reshape(count, X, Y, ZH, 64)
    both_grads = both_grads.transpose(0, 1, 3, 2, 4).reshape(count, 64, 64)
    grad_pooled = jnp.einsum("sij,sje->sie", both_grads, right, preferred_element_type=F32)
    return hidden, (grad_pooled * scale).astype(BF)[:, None]


def solution(mesh):
    fine = Mesh(mesh.devices.reshape(X, ZH, Y, 8), ("x", "zh", "y", "nw"))
    wide = ("x", "zh", "y")
    in_specs = (P(None, "nw", wide, None), P("nw", wide, None), P(), P(wide, "nw"))
    out_specs = (P(wide, "nw"), P(wide, "nw", None, None))
    return jax.shard_map(body, mesh=fine, in_specs=in_specs, out_specs=out_specs, check_vma=False)
```

```python
import jax
import jax.numpy as jnp
from jax import lax
from jax.sharding import Mesh, PartitionSpec as P

X, ZH, Y = 4, 2, 8
XY = X * Y
FIRST = 80
BF = jnp.bfloat16
F32 = jnp.float32


def swap_block(v):
    return lax.ppermute(v, "nw", [(i, i ^ 4) for i in range(8)])


def cross_block(v):
    pairs = [(a * 8 + b, (a ^ 1) * 8 + (b ^ 4)) for a in range(ZH) for b in range(8)]
    return lax.ppermute(v, ("zh", "nw"), pairs)


def cross_same(v):
    return lax.ppermute(v, "zh", [(0, 1), (1, 0)])


def in_order(own, other, zh):
    first = zh == 0
    return jnp.stack([jnp.where(first, own, other), jnp.where(first, other, own)], 0)


def copies_to_all(v, axis):
    sent = jnp.broadcast_to(v[None], (lax.axis_size(axis),) + v.shape)
    return lax.all_to_all(sent, axis, 0, 0, tiled=True)


def along_xy(v):
    return lax.all_to_all(v, ("x", "y"), 0, 0, tiled=True)


def after(v, others, zh):
    for other in others:
        v = jnp.where(zh > 1, other[(0,) * other.ndim].astype(v.dtype), v)
    return v


def folded_weights(w, turned, zh):
    units = w.shape[-1]
    raw_other = cross_same(w)
    near = swap_block(turned)
    far = cross_block(turned)
    theirs = in_order(near, far, zh).transpose(2, 0, 1, 3)
    mine = in_order(w, raw_other, zh).reshape(ZH, X, ZH, Y, units)
    mine = mine.transpose(0, 2, 1, 3, 4).reshape(ZH, ZH, XY, units)
    fold = (mine.astype(F32) + theirs.astype(F32)).astype(BF)
    return fold.reshape(ZH * 64, units)


def body(pooled, w_top, bias, grad_hidden):
    zh = lax.axis_index("zh")
    nw = lax.axis_index("nw")
    half = nw // 4
    count = pooled.shape[0] // (XY * ZH)
    width = pooled.shape[-1]
    units = w_top.shape[-1]
    scale = width ** (-0.5)
    n = FIRST
    rest = count - n

    def my_half(v):
        h = v.shape[1] // 2
        return lax.dynamic_slice_in_dim(v, half * h, h, 1)

    by_dest = pooled.reshape(X, ZH, Y, count, width).transpose(1, 0, 2, 3, 4)
    by_dest = by_dest.reshape(ZH, XY, count, width)
    mine = lax.dynamic_index_in_dim(by_dest, zh, 0, keepdims=False)
    theirs = lax.dynamic_index_in_dim(by_dest, 1 - zh, 0, keepdims=False)

    def move_z(own, away):
        x_away, y_own, y_away = cross_same(my_half(away)), swap_block(own), cross_block(away)
        return my_half(own), x_away, y_own, y_away

    moved_1 = move_z(mine[:, n:], theirs[:, n:])

    w = w_top[0]
    w_rows = w.reshape(X, ZH, Y, units).transpose(0, 2, 1, 3).reshape(XY, -1, width)
    turned = along_xy(w_rows)
    turned_after = after(turned, [moved_1[1]], zh).reshape(XY, ZH, units)
    fold = folded_weights(w, turned_after, zh)
    weights = lax.all_gather(fold, ("x", "y"), axis=0, tiled=True)

    first = jnp.concatenate([mine[:, :n], theirs[:, :n]], 1)
    got = along_xy(after(first, [turned], zh))
    moved_0 = move_z(got[:, :n], got[:, n:])
    last = along_xy(after(jnp.concatenate(moved_1, 1), [got], zh))
    h = rest // 2
    moved_1 = last[:, :h], last[:, h:rest], last[:, rest : 2 * rest], last[:, 2 * rest :]

    cot = copies_to_all(after(grad_hidden, [last], zh), "nw").transpose(1, 0, 2).reshape(count, units)

    def rows_of(own, other):
        v = in_order(own, other, zh).transpose(1, 0, 2, 3)
        return v.reshape(XY * ZH, v.shape[2], width).transpose(1, 0, 2)

    def columns_of(own, other):
        v = in_order(own, other, zh)
        return v.reshape(ZH * XY, v.shape[2], width).transpose(1, 0, 2)

    moved = moved_0, moved_1
    left = jnp.concatenate([rows_of(v[0], v[1]) for v in moved], 0)
    right = [columns_of(v[2], v[3]) for v in moved]
    sizes = [v.shape[0] // 2 for v in right]
    right_half = [lax.dynamic_slice_in_dim(v, half * h, h, 0) for v, h in zip(right, sizes)]
    right, right_half = jnp.concatenate(right, 0), jnp.concatenate(right_half, 0)

    hc = count // 2
    gram = jnp.einsum("sie,sje->sij", left, right_half, preferred_element_type=F32)
    gram = (gram * scale).astype(BF).reshape(hc, 64 * 64)
    part = jnp.dot(gram, weights, preferred_element_type=F32)
    parts = lax.all_gather(part.astype(BF), "nw", axis=0, tiled=False)
    sums = parts.reshape(2, 4, hc, units).astype(F32).sum(1)
    ordered, at = [], 0
    for h in sizes:
        ordered += [sums[0, at : at + h], sums[1, at : at + h]]
        at += h
    pre_act = jnp.concatenate(ordered, 0) + bias[None, :]

    share = grad_hidden.shape[1]
    mine_pre = lax.dynamic_slice_in_dim(pre_act, nw * share, share, 1)
    hidden = jax.nn.silu(mine_pre).astype(BF)
    sig = jax.nn.sigmoid(pre_act)
    grad_pre = (cot.astype(F32) * (sig * (1.0 + pre_act * (1.0 - sig)))).astype(BF)

    rows = lax.dot_general(
        grad_pre, weights, (((1,), (1,)), ((), ())), preferred_element_type=F32
    )
    rows = rows.astype(BF).reshape(count, X, Y, ZH, 64).transpose(0, 1, 3, 2, 4)
    rows = rows.reshape(count, 64, 64)
    grad_pooled = jnp.einsum("sij,sje->sie", rows, right, preferred_element_type=F32)
    return hidden, (grad_pooled * scale).astype(BF)[:, None]


def solution(mesh):
    fine = Mesh(mesh.devices.reshape(X, ZH, Y, 8), ("x", "zh", "y", "nw"))
    wide = ("x", "zh", "y")
    in_specs = (P(None, "nw", wide, None), P("nw", wide, None), P(), P(wide, "nw"))
    out_specs = (P(wide, "nw"), P(wide, "nw", None, None))
    return jax.shard_map(body, mesh=fine, in_specs=in_specs, out_specs=out_specs, check_vma=False)
```

```python
import jax
import jax.numpy as jnp
from jax import lax
from jax.sharding import Mesh, PartitionSpec as P

X, ZH, Y = 4, 2, 8
XY = X * Y
FIRST = 80
BF = jnp.bfloat16
F32 = jnp.float32


def swap_block(v):
    return lax.ppermute(v, "nw", [(i, i ^ 4) for i in range(8)])


def cross_block(v):
    pairs = [(a * 8 + b, (a ^ 1) * 8 + (b ^ 4)) for a in range(ZH) for b in range(8)]
    return lax.ppermute(v, ("zh", "nw"), pairs)


def cross_same(v):
    return lax.ppermute(v, "zh", [(0, 1), (1, 0)])


def in_order(own, other, zh):
    first = zh == 0
    return jnp.stack([jnp.where(first, own, other), jnp.where(first, other, own)], 0)


def along_xy(v):
    return lax.all_to_all(v, ("x", "y"), 0, 0, tiled=True)


def after(v, others, zh):
    for other in others:
        v = jnp.where(zh > 1, other[(0,) * other.ndim].astype(v.dtype), v)
    return v


def folded_weights(w, turned, zh):
    units = w.shape[-1]
    raw_other = cross_same(w)
    near = swap_block(turned)
    far = cross_block(turned)
    theirs = in_order(near, far, zh).transpose(2, 0, 1, 3)
    mine = in_order(w, raw_other, zh).reshape(ZH, X, ZH, Y, units)
    mine = mine.transpose(0, 2, 1, 3, 4).reshape(ZH, ZH, XY, units)
    fold = (mine.astype(F32) + theirs.astype(F32)).astype(BF)
    return fold.reshape(ZH * 64, units)


def body(pooled, w_top, bias, grad_hidden):
    zh = lax.axis_index("zh")
    nw = lax.axis_index("nw")
    half = nw // 4
    count = pooled.shape[0] // (XY * ZH)
    width = pooled.shape[-1]
    units = w_top.shape[-1]
    scale = width ** (-0.5)
    n = FIRST
    rest = count - n

    def my_half(v):
        h = v.shape[1] // 2
        return lax.dynamic_slice_in_dim(v, half * h, h, 1)

    by_dest = pooled.reshape(X, ZH, Y, count, width).transpose(1, 0, 2, 3, 4)
    by_dest = by_dest.reshape(ZH, XY, count, width)
    mine = lax.dynamic_index_in_dim(by_dest, zh, 0, keepdims=False)
    theirs = lax.dynamic_index_in_dim(by_dest, 1 - zh, 0, keepdims=False)

    def move_z(own, away):
        x_away, y_own, y_away = cross_same(my_half(away)), swap_block(own), cross_block(away)
        return my_half(own), x_away, y_own, y_away

    moved_1 = move_z(mine[:, n:], theirs[:, n:])

    w = w_top[0]
    w_rows = w.reshape(X, ZH, Y, units).transpose(0, 2, 1, 3).reshape(XY, ZH, units)
    turned = along_xy(w_rows)
    fold = folded_weights(w, turned, zh)
    weights = lax.all_gather(fold, ("x", "y"), axis=0, tiled=True)

    first = jnp.concatenate([mine[:, :n], theirs[:, :n]], 1)
    got = along_xy(after(first, [turned], zh))
    moved_0 = move_z(got[:, :n], got[:, n:])
    last = along_xy(after(jnp.concatenate(moved_1, 1), [got], zh))
    h = rest // 2
    moved_1 = last[:, :h], last[:, h:rest], last[:, rest : 2 * rest], last[:, 2 * rest :]

    def rows_of(own, other):
        v = in_order(own, other, zh).transpose(1, 0, 2, 3)
        return v.reshape(XY * ZH, v.shape[2], width).transpose(1, 0, 2)

    def columns_of(own, other):
        v = in_order(own, other, zh)
        return v.reshape(ZH * XY, v.shape[2], width).transpose(1, 0, 2)

    moved = moved_0, moved_1
    left = jnp.concatenate([rows_of(v[0], v[1]) for v in moved], 0)
    right = [columns_of(v[2], v[3]) for v in moved]
    sizes = [v.shape[0] // 2 for v in right]
    right_half = [lax.dynamic_slice_in_dim(v, half * h, h, 0) for v, h in zip(right, sizes)]
    right, right_half = jnp.concatenate(right, 0), jnp.concatenate(right_half, 0)

    hc = count // 2
    gram = jnp.einsum("sie,sje->sij", left, right_half, preferred_element_type=F32)
    gram = (gram * scale).astype(BF).reshape(hc, 64 * 64)
    part = jnp.dot(gram, weights, preferred_element_type=F32)
    share = grad_hidden.shape[1]
    cot = grad_hidden.reshape(2, hc, share).transpose(1, 0, 2).reshape(hc, 2 * share)
    parts = lax.all_gather(jnp.concatenate([part.astype(BF), cot], 1), "nw", axis=0, tiled=False)
    sums = parts[:, :, :units].reshape(2, 4, hc, units).astype(F32).sum(1)
    cot = parts[:, :, units:].reshape(8, hc, 2, share).transpose(2, 1, 0, 3)
    cot = cot.reshape(count, units)
    ordered, at = [], 0
    for h in sizes:
        ordered += [sums[0, at : at + h], sums[1, at : at + h]]
        at += h
    pre_act = jnp.concatenate(ordered, 0) + bias[None, :]

    mine_pre = lax.dynamic_slice_in_dim(pre_act, nw * share, share, 1)
    hidden = jax.nn.silu(mine_pre).astype(BF)
    sig = jax.nn.sigmoid(pre_act)
    grad_pre = (cot.astype(F32) * (sig * (1.0 + pre_act * (1.0 - sig)))).astype(BF)

    rows = lax.dot_general(
        grad_pre, weights, (((1,), (1,)), ((), ())), preferred_element_type=F32
    )
    rows = rows.astype(BF).reshape(count, X, Y, ZH, 64).transpose(0, 1, 3, 2, 4)
    rows = rows.reshape(count, 64, 64)
    grad_pooled = jnp.einsum("sij,sje->sie", rows, right, preferred_element_type=F32)
    return hidden, (grad_pooled * scale).astype(BF)[:, None]


def solution(mesh):
    fine = Mesh(mesh.devices.reshape(X, ZH, Y, 8), ("x", "zh", "y", "nw"))
    wide = ("x", "zh", "y")
    in_specs = (P(None, "nw", wide, None), P("nw", wide, None), P(), P(wide, "nw"))
    out_specs = (P(wide, "nw"), P(wide, "nw", None, None))
    return jax.shard_map(body, mesh=fine, in_specs=in_specs, out_specs=out_specs, check_vma=False)
```

```python
import jax
import jax.numpy as jnp
from jax import lax
from jax.sharding import Mesh, PartitionSpec as P

X, ZH, Y = 4, 2, 8
XY = X * Y
FIRST = 80
BF = jnp.bfloat16
F32 = jnp.float32


def swap_block(v):
    return lax.ppermute(v, "nw", [(i, i ^ 4) for i in range(8)])


def cross_block(v):
    pairs = [(a * 8 + b, (a ^ 1) * 8 + (b ^ 4)) for a in range(ZH) for b in range(8)]
    return lax.ppermute(v, ("zh", "nw"), pairs)


def cross_same(v):
    return lax.ppermute(v, "zh", [(0, 1), (1, 0)])


def in_order(own, other, zh):
    first = zh == 0
    return jnp.stack([jnp.where(first, own, other), jnp.where(first, other, own)], 0)


def along_xy(v):
    return lax.all_to_all(v, ("x", "y"), 0, 0, tiled=True)


def folded_weights(w, turned, zh):
    units = w.shape[-1]
    by_zh = w.reshape(X, ZH, Y, units)
    first, second = by_zh[:, 0], by_zh[:, 1]
    raw = in_order(first, second, zh).reshape(ZH * XY, units)
    raw_other = cross_same(in_order(second, first, zh).reshape(ZH * XY, units))
    theirs = jnp.stack([swap_block(turned), cross_block(turned)], 0)
    theirs = theirs.transpose(2, 0, 1, 3)
    mine = in_order(raw, raw_other, zh).reshape(ZH, ZH, XY, units)
    fold = (mine.astype(F32) + theirs.astype(F32)).astype(BF)
    return fold.reshape(ZH * 64, units)


def body(pooled, w_top, bias, grad_hidden):
    zh = lax.axis_index("zh")
    nw = lax.axis_index("nw")
    half = nw // 4
    count = pooled.shape[0] // (XY * ZH)
    width = pooled.shape[-1]
    units = w_top.shape[-1]
    scale = width ** (-0.5)
    n = FIRST
    rest = count - n

    def my_half(v):
        h = v.shape[1] // 2
        return lax.dynamic_slice_in_dim(v, half * h, h, 1)

    by_dest = pooled.reshape(X, ZH, Y, count, width)

    def samples_of(which, start, stop):
        v = lax.dynamic_index_in_dim(by_dest[:, :, :, start:stop], which, 1, keepdims=False)
        return v.reshape(XY, stop - start, width)

    mine = samples_of(zh, 0, n), samples_of(zh, n, count)
    theirs = samples_of(1 - zh, 0, n), samples_of(1 - zh, n, count)

    def move_z(own, away):
        x_away, y_own, y_away = cross_same(my_half(away)), swap_block(own), cross_block(away)
        return my_half(own), x_away, y_own, y_away

    moved_1 = move_z(mine[1], theirs[1])

    w = w_top[0]
    w_rows = w.reshape(X, ZH, Y, units).transpose(0, 2, 1, 3).reshape(XY, ZH, units)
    turned = along_xy(w_rows)
    fold = folded_weights(w, turned, zh)
    weights = lax.all_gather(fold, ("x", "y"), axis=0, tiled=True)

    first = jnp.concatenate([mine[0], theirs[0]], 1)
    got = along_xy(first)
    moved_0 = move_z(got[:, :n], got[:, n:])
    last = along_xy(jnp.concatenate(moved_1, 1))
    h = rest // 2
    moved_1 = last[:, :h], last[:, h:rest], last[:, rest : 2 * rest], last[:, 2 * rest :]

    def rows_of(own, other):
        v = in_order(own, other, zh).transpose(1, 0, 2, 3)
        return v.reshape(XY * ZH, v.shape[2], width).transpose(1, 0, 2)

    def columns_of(own, other):
        return jnp.concatenate([own, other], 0).transpose(1, 0, 2)

    moved = moved_0, moved_1
    left = jnp.concatenate([rows_of(v[0], v[1]) for v in moved], 0)
    right = [columns_of(v[2], v[3]) for v in moved]
    sizes = [v.shape[0] // 2 for v in right]
    right_half = [lax.dynamic_slice_in_dim(v, half * h, h, 0) for v, h in zip(right, sizes)]
    right, right_half = jnp.concatenate(right, 0), jnp.concatenate(right_half, 0)

    hc = count // 2
    gram = jnp.einsum("sie,sje->sij", left, right_half, preferred_element_type=F32)
    gram = (gram * scale).astype(BF).reshape(hc, 64 * 64)
    part = jnp.dot(gram, weights, preferred_element_type=F32)
    share = grad_hidden.shape[1]
    cot = grad_hidden.reshape(2, hc, share).transpose(1, 0, 2).reshape(hc, 2 * share)
    parts = lax.all_gather(jnp.concatenate([part.astype(BF), cot], 1), "nw", axis=0, tiled=False)
    sums = parts[:, :, :units].reshape(2, 4, hc, units).astype(F32).sum(1)
    cot = parts[:, :, units:].reshape(8, hc, 2, share).transpose(2, 1, 0, 3)
    cot = cot.reshape(count, units)
    ordered, at = [], 0
    for h in sizes:
        ordered += [sums[0, at : at + h], sums[1, at : at + h]]
        at += h
    pre_act = jnp.concatenate(ordered, 0) + bias[None, :]

    mine_pre = lax.dynamic_slice_in_dim(pre_act, nw * share, share, 1)
    hidden = jax.nn.silu(mine_pre).astype(BF)
    sig = jax.nn.sigmoid(pre_act)
    grad_pre = (cot.astype(F32) * (sig * (1.0 + pre_act * (1.0 - sig)))).astype(BF)

    rows = lax.dot_general(
        grad_pre, weights, (((1,), (1,)), ((), ())), preferred_element_type=F32
    )
    rows = rows.astype(BF).reshape(count, X, Y, ZH, 64).transpose(0, 1, 3, 2, 4)
    rows = rows.reshape(count, 64, 64)
    grad_pooled = jnp.einsum("sij,sje->sie", rows, right, preferred_element_type=F32)
    return hidden, (grad_pooled * scale).astype(BF)[:, None]


def solution(mesh):
    fine = Mesh(mesh.devices.reshape(X, ZH, Y, 8), ("x", "zh", "y", "nw"))
    wide = ("x", "zh", "y")
    in_specs = (P(None, "nw", wide, None), P("nw", wide, None), P(), P(wide, "nw"))
    out_specs = (P(wide, "nw"), P(wide, "nw", None, None))
    return jax.shard_map(body, mesh=fine, in_specs=in_specs, out_specs=out_specs, check_vma=False)
```

```python
import jax
import jax.numpy as jnp
from jax import lax
from jax.sharding import Mesh, PartitionSpec as P

X, ZH, Y = 4, 2, 8
XY = X * Y
FIRST = 96
BF = jnp.bfloat16
F32 = jnp.float32


def swap_block(v):
    return lax.ppermute(v, "nw", [(i, i ^ 4) for i in range(8)])


def cross_block(v):
    pairs = [(a * 8 + b, (a ^ 1) * 8 + (b ^ 4)) for a in range(ZH) for b in range(8)]
    return lax.ppermute(v, ("zh", "nw"), pairs)


def cross_same(v):
    return lax.ppermute(v, "zh", [(0, 1), (1, 0)])


def in_order(own, other, zh):
    first = zh == 0
    return jnp.stack([jnp.where(first, own, other), jnp.where(first, other, own)], 0)


def along_xy(v):
    return lax.all_to_all(v, ("x", "y"), 0, 0, tiled=True)


def folded_weights(w, turned, zh):
    units = w.shape[-1]
    by_zh = w.reshape(X, ZH, Y, units)
    first, second = by_zh[:, 0], by_zh[:, 1]
    raw = in_order(first, second, zh).reshape(ZH * XY, units)
    raw_other = cross_same(in_order(second, first, zh).reshape(ZH * XY, units))
    theirs = jnp.stack([swap_block(turned), cross_block(turned)], 0)
    theirs = theirs.transpose(2, 0, 1, 3)
    mine = in_order(raw, raw_other, zh).reshape(ZH, ZH, XY, units)
    fold = (mine.astype(F32) + theirs.astype(F32)).astype(BF)
    return fold.reshape(ZH * 64, units)


def body(pooled, w_top, bias, grad_hidden):
    zh = lax.axis_index("zh")
    nw = lax.axis_index("nw")
    half = nw // 4
    count = pooled.shape[0] // (XY * ZH)
    width = pooled.shape[-1]
    units = w_top.shape[-1]
    scale = width ** (-0.5)
    n = FIRST
    rest = count - n

    def my_half(v):
        h = v.shape[1] // 2
        return lax.dynamic_slice_in_dim(v, half * h, h, 1)

    by_dest = pooled.reshape(X, ZH, Y, count, width)

    def samples_of(which, start, stop):
        v = lax.dynamic_index_in_dim(by_dest[:, :, :, start:stop], which, 1, keepdims=False)
        return v.reshape(XY, stop - start, width)

    mine = samples_of(zh, 0, n), samples_of(zh, n, count)
    theirs = samples_of(1 - zh, 0, n), samples_of(1 - zh, n, count)

    def move_z(own, away):
        x_away, y_own, y_away = cross_same(my_half(away)), swap_block(own), cross_block(away)
        return my_half(own), x_away, y_own, y_away

    moved_1 = move_z(mine[1], theirs[1])

    w = w_top[0]
    w_rows = w.reshape(X, ZH, Y, units).transpose(0, 2, 1, 3).reshape(XY, ZH, units)
    turned = along_xy(w_rows)
    fold = folded_weights(w, turned, zh)
    weights = lax.all_gather(fold, ("x", "y"), axis=0, tiled=True)

    first = jnp.concatenate([mine[0], theirs[0]], 1)
    got = along_xy(first)
    moved_0 = move_z(got[:, :n], got[:, n:])
    x_own = jnp.where(zh > 1, got[0, 0, 0], moved_1[0])
    last = along_xy(jnp.concatenate([x_own, *moved_1[1:]], 1))
    h = rest // 2
    moved_1 = last[:, :h], last[:, h:rest], last[:, rest : 2 * rest], last[:, 2 * rest :]

    def rows_of(own, other):
        v = in_order(own, other, zh).transpose(1, 0, 2, 3)
        return v.reshape(XY * ZH, v.shape[2], width).transpose(1, 0, 2)

    def columns_of(own, other):
        return jnp.concatenate([own, other], 0).transpose(1, 0, 2)

    moved = moved_0, moved_1
    left = jnp.concatenate([rows_of(v[0], v[1]) for v in moved], 0)
    right = [columns_of(v[2], v[3]) for v in moved]
    sizes = [v.shape[0] // 2 for v in right]
    right_half = [lax.dynamic_slice_in_dim(v, half * h, h, 0) for v, h in zip(right, sizes)]
    right, right_half = jnp.concatenate(right, 0), jnp.concatenate(right_half, 0)

    hc = count // 2
    gram = jnp.einsum("sie,sje->sij", left, right_half, preferred_element_type=F32)
    gram = (gram * scale).astype(BF).reshape(hc, 64 * 64)
    part = jnp.dot(gram, weights, preferred_element_type=F32)
    share = grad_hidden.shape[1]
    cot = grad_hidden.reshape(2, hc, share).transpose(1, 0, 2).reshape(hc, 2 * share)
    parts = lax.all_gather(jnp.concatenate([part.astype(BF), cot], 1), "nw", axis=0, tiled=False)
    sums = parts[:, :, :units].reshape(2, 4, hc, units).astype(F32).sum(1)
    cot = parts[:, :, units:].reshape(8, hc, 2, share).transpose(2, 1, 0, 3)
    cot = cot.reshape(count, units)
    ordered, at = [], 0
    for h in sizes:
        ordered += [sums[0, at : at + h], sums[1, at : at + h]]
        at += h
    pre_act = jnp.concatenate(ordered, 0) + bias[None, :]

    mine_pre = lax.dynamic_slice_in_dim(pre_act, nw * share, share, 1)
    hidden = jax.nn.silu(mine_pre).astype(BF)
    sig = jax.nn.sigmoid(pre_act)
    grad_pre = (cot.astype(F32) * (sig * (1.0 + pre_act * (1.0 - sig)))).astype(BF)

    rows = lax.dot_general(
        grad_pre, weights, (((1,), (1,)), ((), ())), preferred_element_type=F32
    )
    rows = rows.astype(BF).reshape(count, X, Y, ZH, 64).transpose(0, 1, 3, 2, 4)
    rows = rows.reshape(count, 64, 64)
    grad_pooled = jnp.einsum("sij,sje->sie", rows, right, preferred_element_type=F32)
    return hidden, (grad_pooled * scale).astype(BF)[:, None]


def solution(mesh):
    fine = Mesh(mesh.devices.reshape(X, ZH, Y, 8), ("x", "zh", "y", "nw"))
    wide = ("x", "zh", "y")
    in_specs = (P(None, "nw", wide, None), P("nw", wide, None), P(), P(wide, "nw"))
    out_specs = (P(wide, "nw"), P(wide, "nw", None, None))
    return jax.shard_map(body, mesh=fine, in_specs=in_specs, out_specs=out_specs, check_vma=False)
```

```python
import jax
import jax.numpy as jnp
from jax import lax
from jax.sharding import Mesh, PartitionSpec as P

X, ZH, Y = 4, 2, 8
XY = X * Y
FIRST = 88
BF = jnp.bfloat16
F32 = jnp.float32


def swap_block(v):
    return lax.ppermute(v, "nw", [(i, i ^ 4) for i in range(8)])


def cross_block(v):
    pairs = [(a * 8 + b, (a ^ 1) * 8 + (b ^ 4)) for a in range(ZH) for b in range(8)]
    return lax.ppermute(v, ("zh", "nw"), pairs)


def cross_same(v):
    return lax.ppermute(v, "zh", [(0, 1), (1, 0)])


def in_order(own, other, zh):
    first = zh == 0
    return jnp.stack([jnp.where(first, own, other), jnp.where(first, other, own)], 0)


def along_xy(v):
    return lax.all_to_all(v, ("x", "y"), 0, 0, tiled=True)


def folded_weights(w, turned, zh):
    units = w.shape[-1]
    by_zh = w.reshape(X, ZH, Y, units)
    first, second = by_zh[:, 0], by_zh[:, 1]
    raw = in_order(first, second, zh).reshape(ZH * XY, units)
    raw_other = cross_same(in_order(second, first, zh).reshape(ZH * XY, units))
    theirs = jnp.stack([swap_block(turned), cross_block(turned)], 0)
    theirs = theirs.transpose(2, 0, 1, 3)
    mine = in_order(raw, raw_other, zh).reshape(ZH, ZH, XY, units)
    fold = (mine.astype(F32) + theirs.astype(F32)).astype(BF)
    return fold.reshape(ZH * 64, units)


def body(pooled, w_top, bias, grad_hidden):
    zh = lax.axis_index("zh")
    nw = lax.axis_index("nw")
    half = nw // 4
    count = pooled.shape[0] // (XY * ZH)
    width = pooled.shape[-1]
    units = w_top.shape[-1]
    scale = width ** (-0.5)
    n = FIRST
    rest = count - n

    def my_half(v):
        h = v.shape[1] // 2
        return lax.dynamic_slice_in_dim(v, half * h, h, 1)

    by_dest = pooled.reshape(X, ZH, Y, count, width)

    def samples_of(which, start, stop):
        v = lax.dynamic_index_in_dim(by_dest[:, :, :, start:stop], which, 1, keepdims=False)
        return v.reshape(XY, stop - start, width)

    mine = samples_of(zh, 0, n), samples_of(zh, n, count)
    theirs = samples_of(1 - zh, 0, n), samples_of(1 - zh, n, count)

    def move_z(own, away):
        x_away, y_own, y_away = cross_same(my_half(away)), swap_block(own), cross_block(away)
        return my_half(own), x_away, y_own, y_away

    moved_1 = move_z(mine[1], theirs[1])

    w = w_top[0]
    w_rows = w.reshape(X, ZH, Y, units).transpose(0, 2, 1, 3).reshape(XY, ZH, units)
    turned = along_xy(w_rows)
    fold = folded_weights(w, turned, zh)
    weights = lax.all_gather(fold, ("x", "y"), axis=0, tiled=True)

    first = jnp.concatenate([mine[0], theirs[0]], 1)
    got = along_xy(first)
    moved_0 = move_z(got[:, :n], got[:, n:])
    x_own = jnp.where(zh > 1, got[0, 0, 0], moved_1[0])
    last = along_xy(jnp.concatenate([x_own, *moved_1[1:]], 1))
    h = rest // 2
    moved_1 = last[:, :h], last[:, h:rest], last[:, rest : 2 * rest], last[:, 2 * rest :]

    def rows_of(own, other):
        v = in_order(own, other, zh).transpose(1, 0, 2, 3)
        return v.reshape(XY * ZH, v.shape[2], width).transpose(1, 0, 2)

    def columns_of(own, other):
        return jnp.concatenate([own, other], 0).transpose(1, 0, 2)

    moved = moved_0, moved_1
    left = jnp.concatenate([rows_of(v[0], v[1]) for v in moved], 0)
    right = [columns_of(v[2], v[3]) for v in moved]
    sizes = [v.shape[0] // 2 for v in right]
    right_half = [lax.dynamic_slice_in_dim(v, half * h, h, 0) for v, h in zip(right, sizes)]
    right, right_half = jnp.concatenate(right, 0), jnp.concatenate(right_half, 0)

    hc = count // 2
    gram = jnp.einsum("sie,sje->sij", left, right_half, preferred_element_type=F32)
    gram = (gram * scale).astype(BF).reshape(hc, 64 * 64)
    part = jnp.dot(gram, weights, preferred_element_type=F32)
    share = grad_hidden.shape[1]
    cot = grad_hidden.reshape(2, hc, share).transpose(1, 0, 2).reshape(hc, 2 * share)
    parts = lax.all_gather(jnp.concatenate([part.astype(BF), cot], 1), "nw", axis=0, tiled=False)
    sums = parts[:, :, :units].reshape(2, 4, hc, units).astype(F32).sum(1)
    cot = parts[:, :, units:].reshape(8, hc, 2, share).transpose(2, 1, 0, 3)
    cot = cot.reshape(count, units)
    ordered, at = [], 0
    for h in sizes:
        ordered += [sums[0, at : at + h], sums[1, at : at + h]]
        at += h
    pre_act = jnp.concatenate(ordered, 0) + bias[None, :]

    mine_pre = lax.dynamic_slice_in_dim(pre_act, nw * share, share, 1)
    hidden = jax.nn.silu(mine_pre).astype(BF)
    sig = jax.nn.sigmoid(pre_act)
    grad_pre = (cot.astype(F32) * (sig * (1.0 + pre_act * (1.0 - sig)))).astype(BF)

    rows = lax.dot_general(
        grad_pre, weights, (((1,), (1,)), ((), ())), preferred_element_type=F32
    )
    rows = rows.astype(BF).reshape(count, X, Y, ZH, 64).transpose(0, 1, 3, 2, 4)
    rows = rows.reshape(count, 64, 64)
    grad_pooled = jnp.einsum("sij,sje->sie", rows, right, preferred_element_type=F32)
    return hidden, (grad_pooled * scale).astype(BF)[:, None]


def solution(mesh):
    fine = Mesh(mesh.devices.reshape(X, ZH, Y, 8), ("x", "zh", "y", "nw"))
    wide = ("x", "zh", "y")
    in_specs = (P(None, "nw", wide, None), P("nw", wide, None), P(), P(wide, "nw"))
    out_specs = (P(wide, "nw"), P(wide, "nw", None, None))
    return jax.shard_map(body, mesh=fine, in_specs=in_specs, out_specs=out_specs, check_vma=False)
```
